32 devices in a mesh: grp: 4 (over y, x), slab: 8 (over z, core).
Axes of the slice: x: 2, y: 2, z: 4, core: 2. Of those that a mesh axis runs over, the one named last changes fastest.
Arguments:
- template: float32 [64, 64, 256], P('slab'), may hold values from -6 to 6
- images: bfloat16 [16, 64, 64, 256], P('grp', 'slab'), may hold values from -6 to 6
- velocity: float32 [16, 3, 64, 64, 256], P('grp', None, 'slab'), may hold values from -3 to 3
- labels: int32 [64, 64, 256], P('slab'), may hold values from 0 to 3
- stiffness: float32 [4], replicated, may hold values from 0.5 to 2
- cohort: int32 [16], P('grp'), may hold values from 0 to 7
- site_gain: float32 [8], replicated, may hold values from 0.5 to 2
Outputs:
- new_template: float32 [64, 64, 256], P('slab')
- new_velocity: float32 [16, 3, 64, 64, 256], P('grp', None, 'slab')
The draws below stay inside these ranges and needn't reach their ends.
All inputs are finite; a program needn't handle non-finite values.
Results may differ from the reference program's by a relative error of at most 0.0003.
Values sent between devices are 32-bit elements; how exact they have to be, the bound alone decides.
A program may use at most 64 MiB of HBM per device.

```python
import math
import jax
import jax.numpy as jnp
from jax import lax

NY = 64
NX = 256
NLAB = 4
NCOH = 8
NZ = 64
SUBJ = 16


def plant(array, own_key, smallest, top_value):
    longest = array.shape.index(max(array.shape))
    spots = []
    for shift in (0, 1):
        where = [jax.random.randint(jax.random.fold_in(own_key, axis), (), 0, length) for axis, length in enumerate(array.shape)]
        where[longest] = (where[longest] + shift) % array.shape[longest]
        spots.append(tuple(where))
    return array.at[spots[0]].set(smallest).at[spots[1]].set(top_value)


def block_scale(rng, shape, split, low, largest):
    level, own = 1.0, jax.random.fold_in(rng, 6)
    for axis_at, parts in split:
        heights = jnp.exp(jax.random.uniform(jax.random.fold_in(own, axis_at), (parts,), jnp.float32, low / len(split), largest / len(split)))
        level = level * jnp.repeat(heights, shape[axis_at] // parts).reshape([-1 if axis == axis_at else 1 for axis in range(len(shape))])
    return level


def scatter_about(stream_key, extent, width, limit, pieces=(), kind=jnp.bfloat16):
    array = width * jax.random.normal(stream_key, extent, jnp.float32)
    if pieces:
        array = array * block_scale(stream_key, extent, pieces, -0.22, 0.18)
    return jnp.clip(array, -limit, limit).astype(kind)


def setup_inputs(seed: int = 0) -> dict:
    arg_keys = jax.random.split(jax.random.key(seed), 8)
    template = scatter_about(arg_keys[0], (NZ, NY, NX), 1.0, 6.0, ((0, 8),), jnp.float32)
    images = scatter_about(arg_keys[1], (SUBJ, NZ, NY, NX), 1.0, 6.0, ((0, 4), (1, 8)))
    velocity = scatter_about(arg_keys[2], (SUBJ, 3, NZ, NY, NX), 0.5, 3.0, ((0, 4), (2, 8)), jnp.float32)
    labels = plant(jax.random.randint(arg_keys[3], (NZ, NY, NX), 0, NLAB), jax.random.fold_in(arg_keys[3], 1), 0, NLAB - 1).astype(jnp.int32)
    stiffness = jnp.clip(jnp.exp(jax.random.uniform(arg_keys[4], (NLAB,), jnp.float32, math.log(0.5), math.log(2.0))), 0.5, 2.0)
    cohort = plant(jax.random.randint(arg_keys[5], (SUBJ,), 0, NCOH), jax.random.fold_in(arg_keys[5], 1), 0, NCOH - 1).astype(jnp.int32)
    site_gain = jnp.clip(jnp.exp(jax.random.uniform(arg_keys[6], (NCOH,), jnp.float32, math.log(0.5), math.log(2.0))), 0.5, 2.0)
    return dict(template=template, images=images, velocity=velocity, labels=labels, stiffness=stiffness, cohort=cohort, site_gain=site_gain)


velocity_step = 0.05
template_step = 0.5


def slopes_of(padded):
    along_z = 0.5 * (padded[..., 2:, 1:-1, 1:-1] - padded[..., :-2, 1:-1, 1:-1])
    along_y = 0.5 * (padded[..., 1:-1, 2:, 1:-1] - padded[..., 1:-1, :-2, 1:-1])
    along_x = 0.5 * (padded[..., 1:-1, 1:-1, 2:] - padded[..., 1:-1, 1:-1, :-2])
    return jnp.stack([along_z, along_y, along_x], axis=-4)


def around_of(padded):
    beside_all = padded[..., 2:, 1:-1, 1:-1] + padded[..., :-2, 1:-1, 1:-1]
    beside_all = beside_all + padded[..., 1:-1, 2:, 1:-1] + padded[..., 1:-1, :-2, 1:-1]
    return beside_all + padded[..., 1:-1, 1:-1, 2:] + padded[..., 1:-1, 1:-1, :-2]


def reference(template, images, velocity, labels, stiffness, cohort, site_gain):
    slopes = slopes_of(jnp.pad(template, 1))
    stiff_map = stiffness[labels]
    subject_gain = site_gain[cohort]

    def per_subject(running, inputs):
        image, field, gain = inputs
        residual = template + jnp.sum(slopes * field, axis=0) - gain * image.astype(jnp.float32)
        padded = jnp.pad(field, ((0, 0), (1, 1), (1, 1), (1, 1)))
        elastic = stiff_map * (6.0 * field - around_of(padded))
        moved = field - velocity_step * (residual[None] * slopes + elastic)
        return running + residual, moved

    summed, new_velocity = lax.scan(per_subject, jnp.zeros(template.shape, jnp.float32), (images, velocity, subject_gain))
    return template - template_step * summed / SUBJ, new_velocity
```

```python
import functools

import jax
import jax.numpy as jnp
from jax import lax
from jax.experimental import pallas as pl
from jax.experimental.pallas import tpu as pltpu
from jax.sharding import PartitionSpec as P

velocity_step = 0.05
template_step = 0.5
MESH = pl.DeviceIdType.MESH


def shifted_pair(v, axis):
    size = v.shape[axis]
    spot = lax.broadcasted_iota(jnp.int32, v.shape, axis)
    before = jnp.where(spot == 0, 0.0, pltpu.roll(v, 1, axis))
    after = jnp.where(spot == size - 1, 0.0, pltpu.roll(v, size - 1, axis))
    return before, after


def kernel(
    groups, slabs, split,
    template, images, velocity, labels, stiffness, cohort, site_gain,
    new_template, new_velocity,
    tpad, vpad, img, lab, slope, stiff, resid, part, got, fresh, moved,
    load_sem, vload_sem, iload_sem, out_sem, own_sem,
    tsend, trecv, vsend, vrecv, rs_send, rs_recv, ag_send, ag_recv,
):
    subj, comps, planes, ny, nx = velocity.shape
    share = planes // groups
    me, at = lax.axis_index("grp"), lax.axis_index("slab")
    has_low, has_high = at > 0, at < slabs - 1
    first = lax.rem(me + 1, groups) * share

    def ordered(i):
        return lax.rem(first + i, planes)

    def tload():
        return pltpu.make_async_copy(template, tpad.at[pl.ds(1, planes)], load_sem.at[0])

    def lload():
        return pltpu.make_async_copy(labels, lab, load_sem.at[1])

    def vload(z):
        return pltpu.make_async_copy(velocity.at[:, :, z], vpad.at[:, :, z + 1], vload_sem.at[z])

    def iload(z):
        return pltpu.make_async_copy(images.at[:, z], img.at[:, z], iload_sem.at[z])

    tload().start()
    lload().start()

    @pl.loop(0, planes)
    def _(i):
        z = ordered(i)
        vload(z).start()
        iload(z).start()

    barrier = pltpu.get_barrier_semaphore()

    @pl.when(has_low)
    def _():
        pl.semaphore_signal(barrier, inc=1, device_id={"slab": at - 1}, device_id_type=MESH)

    @pl.when(has_high)
    def _():
        pl.semaphore_signal(barrier, inc=1, device_id={"slab": at + 1}, device_id_type=MESH)

    for d in range(1, groups):
        pl.semaphore_signal(
            barrier, inc=1, device_id={"grp": lax.rem(me + d, groups)}, device_id_type=MESH
        )
    pl.semaphore_wait(
        barrier, groups - 1 + has_low.astype(jnp.int32) + has_high.astype(jnp.int32)
    )

    def to_low(src, dst, send, recv):
        return pltpu.make_async_remote_copy(
            src_ref=src, dst_ref=dst, send_sem=send.at[0], recv_sem=recv.at[0],
            device_id={"slab": at - 1}, device_id_type=MESH,
        )

    def to_high(src, dst, send, recv):
        return pltpu.make_async_remote_copy(
            src_ref=src, dst_ref=dst, send_sem=send.at[1], recv_sem=recv.at[1],
            device_id={"slab": at + 1}, device_id_type=MESH,
        )

    last = planes - 1
    tlow = functools.partial(to_low, template.at[0], tpad.at[planes + 1], tsend, trecv)
    thigh = functools.partial(to_high, template.at[last], tpad.at[0], tsend, trecv)
    vlow = functools.partial(
        to_low, velocity.at[:, :, 0], vpad.at[:, :, planes + 1], vsend, vrecv
    )
    vhigh = functools.partial(
        to_high, velocity.at[:, :, last], vpad.at[:, :, 0], vsend, vrecv
    )

    @pl.when(has_low)
    def _():
        tlow().start()
        vlow().start()

    @pl.when(has_high)
    def _():
        thigh().start()
        vhigh().start()

    @pl.when(jnp.logical_not(has_low))
    def _():
        tpad[0] = jnp.zeros((ny, nx), jnp.float32)
        vpad[:, :, 0] = jnp.zeros((subj, comps, ny, nx), jnp.float32)

    @pl.when(jnp.logical_not(has_high))
    def _():
        tpad[planes + 1] = jnp.zeros((ny, nx), jnp.float32)
        vpad[:, :, planes + 1] = jnp.zeros((subj, comps, ny, nx), jnp.float32)

    tload().wait()
    lload().wait()

    @pl.loop(0, planes)
    def _(z):
        t = tpad[z + 1]
        for axis in (0, 1):
            before, after = shifted_pair(t, axis)
            slope[1 + axis, z] = 0.5 * (after - before)
        level = lab[z]
        k = jnp.zeros((ny, nx), jnp.float32)
        for i in range(stiffness.shape[0]):
            k = jnp.where(level == i, velocity_step * stiffness[i], k)
        stiff[z] = k

    @pl.when(has_high)
    def _():
        to_low(template.at[0], tpad.at[planes + 1], tsend, trecv).wait_recv()

    @pl.when(has_low)
    def _():
        to_high(template.at[last], tpad.at[0], tsend, trecv).wait_recv()

    gains = [site_gain[cohort[s]] for s in range(subj)]

    def rs_copy(z, owner, slot):
        return pltpu.make_async_remote_copy(
            src_ref=part.at[z], dst_ref=got.at[slot, lax.rem(z, share)],
            send_sem=rs_send.at[z], recv_sem=rs_recv.at[slot, lax.rem(z, share)],
            device_id={"grp": owner}, device_id_type=MESH,
        )

    rows = 16

    @pl.loop(0, planes)
    def _(i):
        z = ordered(i)
        vload(z).wait()
        iload(z).wait()
        for y in range(0, ny, rows):
            block = pl.ds(y, rows)
            along_z = 0.5 * (tpad[z + 2, block] - tpad[z, block])
            slope[0, z, block] = along_z
            slopes = [along_z] + [slope[c, z, block] for c in range(1, comps)]
            t = tpad[z + 1, block]
            total = None
            for s in range(subj):
                r = t - gains[s] * img[s, z, block].astype(jnp.float32)
                for c in range(comps):
                    r = r + slopes[c] * vpad[s, c, z + 1, block]
                resid[s, z, block] = r
                total = r if total is None else total + r
            part[z, block] = total
        owner = lax.div(z, share)

        @pl.when(owner != me)
        def _():
            rs_copy(z, owner, lax.rem(me - owner + groups, groups) - 1).start()

    def vout(z):
        return pltpu.make_async_copy(moved.at[:, :, z], new_velocity.at[:, :, z], out_sem.at[z])

    def update(z):
        k = stiff[z]
        keep = 1.0 - 6.0 * k
        push = [velocity_step * slope[c, z] for c in range(comps)]

        @pl.loop(0, subj)
        def _(s):
            r = resid[s, z]
            for c in range(comps):
                v = vpad[s, c, z + 1]
                up, down = shifted_pair(v, 0)
                left, right = shifted_pair(v, 1)
                beside = (vpad[s, c, z] + vpad[s, c, z + 2]) + ((up + down) + (left + right))
                moved[s, c, z] = keep * v - r * push[c] + k * beside

        vout(z).start()

    @pl.loop(1, split)
    def _(z):
        update(z)

    subjects = subj * groups

    def ag_copy(j, d):
        peer = lax.rem(me + d, groups)
        slot = groups - d - 1
        return pltpu.make_async_remote_copy(
            src_ref=fresh.at[j], dst_ref=new_template.at[me * share + j],
            send_sem=ag_send.at[j, d - 1], recv_sem=ag_recv.at[slot, j],
            device_id={"grp": peer}, device_id_type=MESH,
        )

    def ag_arrival(j, slot):
        sender = lax.rem(me + slot + 1, groups)
        return pltpu.make_async_remote_copy(
            src_ref=fresh.at[j], dst_ref=new_template.at[sender * share + j],
            send_sem=ag_send.at[j, 0], recv_sem=ag_recv.at[slot, j],
            device_id={"grp": sender}, device_id_type=MESH,
        )

    def own_copy(j):
        return pltpu.make_async_copy(fresh.at[j], new_template.at[me * share + j], own_sem.at[j])

    for j in range(share):
        z = me * share + j
        total = part[z]
        for slot in range(groups - 1):
            rs_copy(z, lax.rem(me + 1, groups), slot).wait_recv()
            total = total + got[slot, j]
        fresh[j] = tpad[z + 1] - (template_step / subjects) * total
        for d in range(1, groups):
            ag_copy(j, d).start()
        own_copy(j).start()

    @pl.loop(split, last)
    def _(z):
        update(z)

    @pl.when(has_low)
    def _():
        vhigh().wait_recv()

    update(0)

    @pl.when(has_high)
    def _():
        vlow().wait_recv()

    update(last)

    @pl.when(has_low)
    def _():
        tlow().wait_send()
        vlow().wait_send()

    @pl.when(has_high)
    def _():
        thigh().wait_send()
        vhigh().wait_send()

    @pl.loop(0, planes)
    def _(z):
        owner = lax.div(z, share)

        @pl.when(owner != me)
        def _():
            rs_copy(z, owner, lax.rem(me - owner + groups, groups) - 1).wait_send()

        vout(z).wait()

    for j in range(share):
        own_copy(j).wait()
        for d in range(1, groups):
            ag_copy(j, d).wait_send()
            ag_arrival(j, d - 1).wait_recv()


def local(template, images, velocity, labels, stiffness, cohort, site_gain):
    groups, slabs = lax.axis_size("grp"), lax.axis_size("slab")
    subj, comps, planes, ny, nx = velocity.shape
    share = planes // groups
    f32, dma = jnp.float32, pltpu.SemaphoreType.DMA
    anywhere = pl.BlockSpec(memory_space=pl.ANY)
    scalars = pl.BlockSpec(memory_space=pltpu.SMEM)
    size = velocity.size
    return pl.pallas_call(
        functools.partial(kernel, groups, slabs, planes // 2 + 1),
        out_shape=(
            jax.ShapeDtypeStruct(template.shape, f32),
            jax.ShapeDtypeStruct(velocity.shape, f32),
        ),
        in_specs=[anywhere] * 4 + [scalars] * 3,
        out_specs=(anywhere, anywhere),
        scratch_shapes=[
            pltpu.VMEM((planes + 2, ny, nx), f32),
            pltpu.VMEM((subj, comps, planes + 2, ny, nx), f32),
            pltpu.VMEM((subj, planes, ny, nx), images.dtype),
            pltpu.VMEM((planes, ny, nx), jnp.int32),
            pltpu.VMEM((comps, planes, ny, nx), f32),
            pltpu.VMEM((planes, ny, nx), f32),
            pltpu.VMEM((subj, planes, ny, nx), f32),
            pltpu.VMEM((planes, ny, nx), f32),
            pltpu.VMEM((groups - 1, share, ny, nx), f32),
            pltpu.VMEM((share, ny, nx), f32),
            pltpu.VMEM((subj, comps, planes, ny, nx), f32),
            dma((2,)), dma((planes,)), dma((planes,)), dma((planes,)), dma((share,)),
            dma((2,)), dma((2,)), dma((2,)), dma((2,)),
            dma((planes,)), dma((groups - 1, share)),
            dma((share, groups - 1)), dma((groups - 1, share)),
        ],
        compiler_params=pltpu.CompilerParams(
            collective_id=0, has_side_effects=True, vmem_limit_bytes=40 * 2**20
        ),
        cost_estimate=pl.CostEstimate(
            flops=24 * size, bytes_accessed=9 * size, transcendentals=0
        ),
    )(template, images, velocity, labels, stiffness, cohort, site_gain)


def solution(mesh):
    placed = (
        P("slab", None, None),
        P("grp", "slab", None, None),
        P("grp", None, "slab", None, None),
        P("slab", None, None),
        P(),
        P("grp"),
        P(),
    )
    return jax.shard_map(
        local,
        mesh=mesh,
        in_specs=placed,
        out_specs=(P("slab", None, None), P("grp", None, "slab", None, None)),
        check_vma=False,
    )
```

```python
import functools

import jax
import jax.numpy as jnp
from jax import lax
from jax.experimental import pallas as pl
from jax.experimental.pallas import tpu as pltpu
from jax.sharding import PartitionSpec as P

velocity_step = 0.05
template_step = 0.5
MESH = pl.DeviceIdType.MESH


def shifted_pair(v, axis):
    size = v.shape[axis]
    spot = lax.broadcasted_iota(jnp.int32, v.shape, axis)
    before = jnp.where(spot == 0, 0.0, pltpu.roll(v, 1, axis))
    after = jnp.where(spot == size - 1, 0.0, pltpu.roll(v, size - 1, axis))
    return before, after


def kernel(
    groups, slabs, split,
    template, images, velocity, labels, stiffness_in, cohort_in, site_gain_in,
    new_template, moved,
    stiffness, cohort, site_gain,
    tpad, vpad, img, lab, slope, stiff, resid, part, got,
    load_sem, vload_sem, iload_sem,
    tsend, trecv, vsend, vrecv, rs_send, rs_recv, ag_send, ag_recv,
):
    subj, comps, planes, ny, nx = velocity.shape
    share = planes // groups
    me, at = lax.axis_index("grp"), lax.axis_index("slab")
    has_low, has_high = at > 0, at < slabs - 1
    first = lax.rem(me + 1, groups) * share

    def ordered(i):
        return lax.rem(first + i, planes)

    def tload():
        return pltpu.make_async_copy(template, tpad.at[pl.ds(1, planes)], load_sem.at[0])

    def lload():
        return pltpu.make_async_copy(labels, lab, load_sem.at[1])

    def vload(z):
        return pltpu.make_async_copy(velocity.at[:, :, z], vpad.at[:, :, z + 1], vload_sem.at[z])

    def iload(z):
        return pltpu.make_async_copy(images.at[:, z], img.at[:, z], iload_sem.at[z])

    def scalar_loads():
        pairs = ((stiffness_in, stiffness), (cohort_in, cohort), (site_gain_in, site_gain))
        return [pltpu.make_async_copy(a, b, load_sem.at[2 + i]) for i, (a, b) in enumerate(pairs)]

    tload().start()
    lload().start()
    for load in scalar_loads():
        load.start()

    @pl.loop(0, planes)
    def _(i):
        z = ordered(i)
        vload(z).start()
        iload(z).start()

    barrier = pltpu.get_barrier_semaphore()

    @pl.when(has_low)
    def _():
        pl.semaphore_signal(barrier, inc=1, device_id={"slab": at - 1}, device_id_type=MESH)

    @pl.when(has_high)
    def _():
        pl.semaphore_signal(barrier, inc=1, device_id={"slab": at + 1}, device_id_type=MESH)

    for d in range(1, groups):
        pl.semaphore_signal(
            barrier, inc=1, device_id={"grp": lax.rem(me + d, groups)}, device_id_type=MESH
        )
    pl.semaphore_wait(
        barrier, groups - 1 + has_low.astype(jnp.int32) + has_high.astype(jnp.int32)
    )

    def to_low(src, dst, send, recv):
        return pltpu.make_async_remote_copy(
            src_ref=src, dst_ref=dst, send_sem=send.at[0], recv_sem=recv.at[0],
            device_id={"slab": at - 1}, device_id_type=MESH,
        )

    def to_high(src, dst, send, recv):
        return pltpu.make_async_remote_copy(
            src_ref=src, dst_ref=dst, send_sem=send.at[1], recv_sem=recv.at[1],
            device_id={"slab": at + 1}, device_id_type=MESH,
        )

    last = planes - 1
    tlow = functools.partial(to_low, template.at[0], tpad.at[planes + 1], tsend, trecv)
    thigh = functools.partial(to_high, template.at[last], tpad.at[0], tsend, trecv)
    vlow = functools.partial(
        to_low, velocity.at[:, :, 0], vpad.at[:, :, planes + 1], vsend, vrecv
    )
    vhigh = functools.partial(
        to_high, velocity.at[:, :, last], vpad.at[:, :, 0], vsend, vrecv
    )

    @pl.when(has_low)
    def _():
        tlow().start()
        vlow().start()

    @pl.when(has_high)
    def _():
        thigh().start()
        vhigh().start()

    @pl.when(jnp.logical_not(has_low))
    def _():
        tpad[0] = jnp.zeros((ny, nx), jnp.float32)
        vpad[:, :, 0] = jnp.zeros((subj, comps, ny, nx), jnp.float32)

    @pl.when(jnp.logical_not(has_high))
    def _():
        tpad[planes + 1] = jnp.zeros((ny, nx), jnp.float32)
        vpad[:, :, planes + 1] = jnp.zeros((subj, comps, ny, nx), jnp.float32)

    tload().wait()
    lload().wait()
    for load in scalar_loads():
        load.wait()

    @pl.loop(0, planes)
    def _(z):
        t = tpad[z + 1]
        for axis in (0, 1):
            before, after = shifted_pair(t, axis)
            slope[1 + axis, z] = 0.5 * (after - before)
        level = lab[z]
        k = jnp.zeros((ny, nx), jnp.float32)
        for i in range(stiffness.shape[0]):
            k = jnp.where(level == i, velocity_step * stiffness[i], k)
        stiff[z] = k

    @pl.when(has_high)
    def _():
        to_low(template.at[0], tpad.at[planes + 1], tsend, trecv).wait_recv()

    @pl.when(has_low)
    def _():
        to_high(template.at[last], tpad.at[0], tsend, trecv).wait_recv()

    gains = [site_gain[cohort[s]] for s in range(subj)]

    def rs_copy(z, owner, slot):
        return pltpu.make_async_remote_copy(
            src_ref=part.at[z], dst_ref=got.at[slot, lax.rem(z, share)],
            send_sem=rs_send.at[z], recv_sem=rs_recv.at[slot, lax.rem(z, share)],
            device_id={"grp": owner}, device_id_type=MESH,
        )

    rows = 16

    @pl.loop(0, planes)
    def _(i):
        z = ordered(i)
        vload(z).wait()
        iload(z).wait()
        for y in range(0, ny, rows):
            block = pl.ds(y, rows)
            along_z = 0.5 * (tpad[z + 2, block] - tpad[z, block])
            slope[0, z, block] = along_z
            slopes = [along_z] + [slope[c, z, block] for c in range(1, comps)]
            t = tpad[z + 1, block]
            total = None
            for s in range(subj):
                r = t - gains[s] * img[s, z, block].astype(jnp.float32)
                for c in range(comps):
                    r = r + slopes[c] * vpad[s, c, z + 1, block]
                resid[s, z, block] = r
                total = r if total is None else total + r
            part[z, block] = total
        owner = lax.div(z, share)

        @pl.when(owner != me)
        def _():
            rs_copy(z, owner, lax.rem(me - owner + groups, groups) - 1).start()

    def update(z):
        k = stiff[z]
        keep = 1.0 - 6.0 * k
        push = [velocity_step * slope[c, z] for c in range(comps)]

        @pl.loop(0, subj)
        def _(s):
            r = resid[s, z]
            for c in range(comps):
                v = vpad[s, c, z + 1]
                up, down = shifted_pair(v, 0)
                left, right = shifted_pair(v, 1)
                beside = (vpad[s, c, z] + vpad[s, c, z + 2]) + ((up + down) + (left + right))
                moved[s, c, z] = keep * v - r * push[c] + k * beside


    @pl.loop(1, split)
    def _(z):
        update(z)

    subjects = subj * groups

    def ag_copy(j, d):
        peer = lax.rem(me + d, groups)
        slot = groups - d - 1
        return pltpu.make_async_remote_copy(
            src_ref=new_template.at[me * share + j], dst_ref=new_template.at[me * share + j],
            send_sem=ag_send.at[j, d - 1], recv_sem=ag_recv.at[slot, j],
            device_id={"grp": peer}, device_id_type=MESH,
        )

    def ag_arrival(j, slot):
        sender = lax.rem(me + slot + 1, groups)
        return pltpu.make_async_remote_copy(
            src_ref=new_template.at[sender * share + j], dst_ref=new_template.at[sender * share + j],
            send_sem=ag_send.at[j, 0], recv_sem=ag_recv.at[slot, j],
            device_id={"grp": sender}, device_id_type=MESH,
        )

    for j in range(share):
        z = me * share + j
        total = part[z]
        for slot in range(groups - 1):
            rs_copy(z, lax.rem(me + 1, groups), slot).wait_recv()
            total = total + got[slot, j]
        new_template[z] = tpad[z + 1] - (template_step / subjects) * total
        for d in range(1, groups):
            ag_copy(j, d).start()

    @pl.loop(split, last)
    def _(z):
        update(z)

    @pl.when(has_low)
    def _():
        vhigh().wait_recv()

    update(0)

    @pl.when(has_high)
    def _():
        vlow().wait_recv()

    update(last)

    @pl.when(has_low)
    def _():
        tlow().wait_send()
        vlow().wait_send()

    @pl.when(has_high)
    def _():
        thigh().wait_send()
        vhigh().wait_send()

    @pl.loop(0, planes)
    def _(z):
        owner = lax.div(z, share)

        @pl.when(owner != me)
        def _():
            rs_copy(z, owner, lax.rem(me - owner + groups, groups) - 1).wait_send()

    for j in range(share):
        for d in range(1, groups):
            ag_copy(j, d).wait_send()
            ag_arrival(j, d - 1).wait_recv()


def handed_on(template, velocity, new_template, new_velocity, sem):
    copies = [
        pltpu.make_async_copy(velocity, new_velocity, sem.at[0]),
        pltpu.make_async_copy(template, new_template, sem.at[1]),
    ]
    for copy in copies:
        copy.start()
    for copy in copies:
        copy.wait()


def local(template, images, velocity, labels, stiffness, cohort, site_gain):
    groups, slabs = lax.axis_size("grp"), lax.axis_size("slab")
    subj, comps, planes, ny, nx = velocity.shape
    share = planes // groups
    f32, dma = jnp.float32, pltpu.SemaphoreType.DMA
    hbm = pl.BlockSpec(memory_space=pltpu.HBM)
    vmem = pl.BlockSpec(memory_space=pltpu.VMEM)
    size = velocity.size
    held = pl.pallas_call(
        functools.partial(kernel, groups, slabs, planes // 2 + 1),
        out_shape=(
            pltpu.VMEM(template.shape, f32),
            pltpu.VMEM(velocity.shape, f32),
        ),
        in_specs=[hbm] * 7,
        out_specs=(vmem, vmem),
        scratch_shapes=[
            pltpu.SMEM(stiffness.shape, f32),
            pltpu.SMEM(cohort.shape, jnp.int32),
            pltpu.SMEM(site_gain.shape, f32),
            pltpu.VMEM((planes + 2, ny, nx), f32),
            pltpu.VMEM((subj, comps, planes + 2, ny, nx), f32),
            pltpu.VMEM((subj, planes, ny, nx), images.dtype),
            pltpu.VMEM((planes, ny, nx), jnp.int32),
            pltpu.VMEM((comps, planes, ny, nx), f32),
            pltpu.VMEM((planes, ny, nx), f32),
            pltpu.VMEM((subj, planes, ny, nx), f32),
            pltpu.VMEM((planes, ny, nx), f32),
            pltpu.VMEM((groups - 1, share, ny, nx), f32),
            dma((5,)), dma((planes,)), dma((planes,)),
            dma((2,)), dma((2,)), dma((2,)), dma((2,)),
            dma((planes,)), dma((groups - 1, share)),
            dma((share, groups - 1)), dma((groups - 1, share)),
        ],
        compiler_params=pltpu.CompilerParams(
            collective_id=0, has_side_effects=True, vmem_limit_bytes=40 * 2**20
        ),
        cost_estimate=pl.CostEstimate(
            flops=24 * size, bytes_accessed=9 * size, transcendentals=0
        ),
    )(
        *(
            pltpu.with_memory_space_constraint(x, pltpu.HBM)
            for x in (template, images, velocity, labels, stiffness, cohort, site_gain)
        )
    )
    return pl.pallas_call(
        handed_on,
        out_shape=(
            jax.ShapeDtypeStruct(template.shape, f32),
            jax.ShapeDtypeStruct(velocity.shape, f32),
        ),
        in_specs=[vmem] * 2,
        out_specs=(hbm, hbm),
        scratch_shapes=[dma((2,))],
        compiler_params=pltpu.CompilerParams(vmem_limit_bytes=24 * 2**20),
        cost_estimate=pl.CostEstimate(flops=0, bytes_accessed=4 * size, transcendentals=0),
    )(*held)


def solution(mesh):
    placed = (
        P("slab", None, None),
        P("grp", "slab", None, None),
        P("grp", None, "slab", None, None),
        P("slab", None, None),
        P(),
        P("grp"),
        P(),
    )
    return jax.shard_map(
        local,
        mesh=mesh,
        in_specs=placed,
        out_specs=(P("slab", None, None), P("grp", None, "slab", None, None)),
        check_vma=False,
    )
```

```python
import functools

import jax
import jax.numpy as jnp
from jax import lax
from jax.experimental import pallas as pl
from jax.experimental.pallas import tpu as pltpu
from jax.sharding import PartitionSpec as P

velocity_step = 0.05
template_step = 0.5
MESH = pl.DeviceIdType.MESH


def shifted_pair(v, axis):
    size = v.shape[axis]
    spot = lax.broadcasted_iota(jnp.int32, v.shape, axis)
    before = jnp.where(spot == 0, 0.0, pltpu.roll(v, 1, axis))
    after = jnp.where(spot == size - 1, 0.0, pltpu.roll(v, size - 1, axis))
    return before, after


def kernel(
    groups, slabs, split,
    template, images, velocity, labels, stiffness_in, cohort_in, site_gain_in,
    new_template, moved,
    stiffness, cohort, site_gain,
    tpad, vpad, img, lab, slope, stiff, resid, part, got,
    load_sem, vload_sem, iload_sem,
    tsend, trecv, vsend, vrecv, rs_send, rs_recv, ag_send, ag_recv,
):
    subj, comps, planes, ny, nx = velocity.shape
    share = planes // groups
    me, at = lax.axis_index("grp"), lax.axis_index("slab")
    has_low, has_high = at > 0, at < slabs - 1
    relay = groups == 4 and share == 2
    first = lax.rem(me + 1, groups) * share
    beside_x, beside_y, across = me + 1 - 2 * lax.rem(me, 2), lax.rem(me + 2, 4), 3 - me
    hops = [
        (2 * across, beside_x), (2 * across + 1, beside_y),
        (2 * beside_x, beside_x), (2 * beside_y + 1, beside_y),
        (2 * beside_x + 1, beside_x), (2 * beside_y, beside_y),
    ]
    order = [z for z, _ in hops] + [2 * me, 2 * me + 1]
    gathers = [
        (2 * me, beside_x), (2 * me + 1, beside_y),
        (2 * me + 1, beside_x), (2 * me, beside_y),
        (2 * beside_x, beside_y), (2 * beside_y + 1, beside_x),
    ]
    arrivals = [
        (2 * beside_x, beside_x), (2 * beside_y + 1, beside_y),
        (2 * beside_x + 1, beside_x), (2 * beside_y, beside_y),
        (2 * across, beside_y), (2 * across + 1, beside_x),
    ]

    def ordered(i):
        return lax.rem(first + i, planes)

    def tload():
        return pltpu.make_async_copy(template, tpad.at[pl.ds(1, planes)], load_sem.at[0])

    def lload():
        return pltpu.make_async_copy(labels, lab, load_sem.at[1])

    def vload(z):
        return pltpu.make_async_copy(velocity.at[:, :, z], vpad.at[:, :, z + 1], vload_sem.at[z])

    def iload(z):
        return pltpu.make_async_copy(images.at[:, z], img.at[:, z], iload_sem.at[z])

    def scalar_loads():
        pairs = ((stiffness_in, stiffness), (cohort_in, cohort), (site_gain_in, site_gain))
        return [pltpu.make_async_copy(a, b, load_sem.at[2 + i]) for i, (a, b) in enumerate(pairs)]

    tload().start()
    lload().start()
    for load in scalar_loads():
        load.start()

    for i in range(planes):
        z = order[i] if relay else ordered(i)
        vload(z).start()
        iload(z).start()

    barrier = pltpu.get_barrier_semaphore()

    @pl.when(has_low)
    def _():
        pl.semaphore_signal(barrier, inc=1, device_id={"slab": at - 1}, device_id_type=MESH)

    @pl.when(has_high)
    def _():
        pl.semaphore_signal(barrier, inc=1, device_id={"slab": at + 1}, device_id_type=MESH)

    for d in range(1, groups):
        pl.semaphore_signal(
            barrier, inc=1, device_id={"grp": lax.rem(me + d, groups)}, device_id_type=MESH
        )
    pl.semaphore_wait(
        barrier, groups - 1 + has_low.astype(jnp.int32) + has_high.astype(jnp.int32)
    )

    def to_low(src, dst, send, recv):
        return pltpu.make_async_remote_copy(
            src_ref=src, dst_ref=dst, send_sem=send.at[0], recv_sem=recv.at[0],
            device_id={"slab": at - 1}, device_id_type=MESH,
        )

    def to_high(src, dst, send, recv):
        return pltpu.make_async_remote_copy(
            src_ref=src, dst_ref=dst, send_sem=send.at[1], recv_sem=recv.at[1],
            device_id={"slab": at + 1}, device_id_type=MESH,
        )

    last = planes - 1
    tlow = functools.partial(to_low, template.at[0], tpad.at[planes + 1], tsend, trecv)
    thigh = functools.partial(to_high, template.at[last], tpad.at[0], tsend, trecv)
    vlow = functools.partial(
        to_low, velocity.at[:, :, 0], vpad.at[:, :, planes + 1], vsend, vrecv
    )
    vhigh = functools.partial(
        to_high, velocity.at[:, :, last], vpad.at[:, :, 0], vsend, vrecv
    )

    @pl.when(has_low)
    def _():
        tlow().start()
        vlow().start()

    @pl.when(has_high)
    def _():
        thigh().start()
        vhigh().start()

    @pl.when(jnp.logical_not(has_low))
    def _():
        tpad[0] = jnp.zeros((ny, nx), jnp.float32)
        vpad[:, :, 0] = jnp.zeros((subj, comps, ny, nx), jnp.float32)

    @pl.when(jnp.logical_not(has_high))
    def _():
        tpad[planes + 1] = jnp.zeros((ny, nx), jnp.float32)
        vpad[:, :, planes + 1] = jnp.zeros((subj, comps, ny, nx), jnp.float32)

    tload().wait()
    lload().wait()
    for load in scalar_loads():
        load.wait()

    @pl.loop(0, planes)
    def _(z):
        t = tpad[z + 1]
        for axis in (0, 1):
            before, after = shifted_pair(t, axis)
            slope[1 + axis, z] = 0.5 * (after - before)
        level = lab[z]
        k = jnp.zeros((ny, nx), jnp.float32)
        for i in range(stiffness.shape[0]):
            k = jnp.where(level == i, velocity_step * stiffness[i], k)
        stiff[z] = k

    @pl.when(has_high)
    def _():
        to_low(template.at[0], tpad.at[planes + 1], tsend, trecv).wait_recv()

    @pl.when(has_low)
    def _():
        to_high(template.at[last], tpad.at[0], tsend, trecv).wait_recv()

    gains = [site_gain[cohort[s]] for s in range(subj)]

    def rs_copy(z, owner, slot):
        return pltpu.make_async_remote_copy(
            src_ref=part.at[z], dst_ref=got.at[slot * share + lax.rem(z, share)],
            send_sem=rs_send.at[z], recv_sem=rs_recv.at[slot * share + lax.rem(z, share)],
            device_id={"grp": owner}, device_id_type=MESH,
        )

    rows = 16

    def residual_plane(z):
        vload(z).wait()
        iload(z).wait()
        for y in range(0, ny, rows):
            block = pl.ds(y, rows)
            along_z = 0.5 * (tpad[z + 2, block] - tpad[z, block])
            slope[0, z, block] = along_z
            slopes = [along_z] + [slope[c, z, block] for c in range(1, comps)]
            t = tpad[z + 1, block]
            total = None
            for s in range(subj):
                r = t - gains[s] * img[s, z, block].astype(jnp.float32)
                for c in range(comps):
                    r = r + slopes[c] * vpad[s, c, z + 1, block]
                resid[s, z, block] = r
                total = r if total is None else total + r
            part[z, block] = total

    def hop(i, src, dst, peer, send, recv):
        return pltpu.make_async_remote_copy(
            src_ref=src, dst_ref=dst, send_sem=send.at[i], recv_sem=recv.at[i],
            device_id={"grp": peer}, device_id_type=MESH,
        )

    def reduce_hop(i):
        z, peer = hops[i]
        return hop(i, part.at[z], got.at[i], peer, rs_send, rs_recv)

    def gather_hop(i):
        z, peer = gathers[i]
        return hop(i, new_template.at[z], new_template.at[z], peer, ag_send, ag_recv)

    def gather_arrival(i):
        z, peer = arrivals[i]
        return hop(i, new_template.at[z], new_template.at[z], peer, ag_send, ag_recv)

    if relay:
        for i, z in enumerate(order):
            residual_plane(z)
            if i < 4:
                reduce_hop(i).start()
        for i, via in ((4, 1), (5, 0)):
            z = hops[i][0]
            reduce_hop(via).wait_recv()
            part[z] = part[z] + got[via]
            reduce_hop(i).start()
    else:
        @pl.loop(0, planes)
        def _(i):
            z = ordered(i)
            residual_plane(z)
            owner = lax.div(z, share)

            @pl.when(owner != me)
            def _():
                rs_copy(z, owner, lax.rem(me - owner + groups, groups) - 1).start()

    def update(z):
        k = stiff[z]
        keep = 1.0 - 6.0 * k
        push = [velocity_step * slope[c, z] for c in range(comps)]

        @pl.loop(0, subj)
        def _(s):
            r = resid[s, z]
            for c in range(comps):
                v = vpad[s, c, z + 1]
                up, down = shifted_pair(v, 0)
                left, right = shifted_pair(v, 1)
                beside = (vpad[s, c, z] + vpad[s, c, z + 2]) + ((up + down) + (left + right))
                moved[s, c, z] = keep * v - r * push[c] + k * beside


    @pl.loop(1, split)
    def _(z):
        update(z)

    subjects = subj * groups

    def ag_copy(j, d):
        peer = lax.rem(me + d, groups)
        slot = groups - d - 1
        return pltpu.make_async_remote_copy(
            src_ref=new_template.at[me * share + j], dst_ref=new_template.at[me * share + j],
            send_sem=ag_send.at[j * (groups - 1) + d - 1], recv_sem=ag_recv.at[slot * share + j],
            device_id={"grp": peer}, device_id_type=MESH,
        )

    def ag_arrival(j, slot):
        sender = lax.rem(me + slot + 1, groups)
        return pltpu.make_async_remote_copy(
            src_ref=new_template.at[sender * share + j], dst_ref=new_template.at[sender * share + j],
            send_sem=ag_send.at[j], recv_sem=ag_recv.at[slot * share + j],
            device_id={"grp": sender}, device_id_type=MESH,
        )

    if relay:
        for j, sources in ((0, (2, 5)), (1, (3, 4))):
            z = 2 * me + j
            total = part[z]
            for i in sources:
                reduce_hop(i).wait_recv()
                total = total + got[i]
            new_template[z] = tpad[z + 1] - (template_step / subjects) * total
            gather_hop(j).start()
        gather_hop(2).start()
        gather_hop(3).start()
    else:
        for j in range(share):
            z = me * share + j
            total = part[z]
            for slot in range(groups - 1):
                rs_copy(z, lax.rem(me + 1, groups), slot).wait_recv()
                total = total + got[slot * share + j]
            new_template[z] = tpad[z + 1] - (template_step / subjects) * total
            for d in range(1, groups):
                ag_copy(j, d).start()

    @pl.loop(split, last)
    def _(z):
        update(z)

    if relay:
        for i in (0, 1):
            gather_arrival(i).wait_recv()
            gather_hop(i + 4).start()

    @pl.when(has_low)
    def _():
        vhigh().wait_recv()

    update(0)

    @pl.when(has_high)
    def _():
        vlow().wait_recv()

    update(last)

    @pl.when(has_low)
    def _():
        tlow().wait_send()
        vlow().wait_send()

    @pl.when(has_high)
    def _():
        thigh().wait_send()
        vhigh().wait_send()

    if relay:
        for i in range(6):
            reduce_hop(i).wait_send()
            gather_hop(i).wait_send()
        for i in range(2, 6):
            gather_arrival(i).wait_recv()
    else:
        @pl.loop(0, planes)
        def _(z):
            owner = lax.div(z, share)

            @pl.when(owner != me)
            def _():
                rs_copy(z, owner, lax.rem(me - owner + groups, groups) - 1).wait_send()

        for j in range(share):
            for d in range(1, groups):
                ag_copy(j, d).wait_send()
                ag_arrival(j, d - 1).wait_recv()


def handed_on(template, velocity, new_template, new_velocity, sem):
    subj, comps = velocity.shape[:2]
    copies = [
        pltpu.make_async_copy(velocity.at[s, c], new_velocity.at[s, c], sem.at[s * comps + c])
        for s in range(subj)
        for c in range(comps)
    ]
    copies.append(pltpu.make_async_copy(template, new_template, sem.at[subj * comps]))
    for copy in copies:
        copy.start()
    for copy in copies:
        copy.wait()


def local(template, images, velocity, labels, stiffness, cohort, site_gain):
    groups, slabs = lax.axis_size("grp"), lax.axis_size("slab")
    subj, comps, planes, ny, nx = velocity.shape
    others = (groups - 1) * (planes // groups)
    f32, dma = jnp.float32, pltpu.SemaphoreType.DMA
    hbm = pl.BlockSpec(memory_space=pltpu.HBM)
    vmem = pl.BlockSpec(memory_space=pltpu.VMEM)
    size = velocity.size
    held = pl.pallas_call(
        functools.partial(kernel, groups, slabs, planes // 2 + 1),
        out_shape=(
            pltpu.VMEM(template.shape, f32),
            pltpu.VMEM(velocity.shape, f32),
        ),
        in_specs=[hbm] * 7,
        out_specs=(vmem, vmem),
        scratch_shapes=[
            pltpu.SMEM(stiffness.shape, f32),
            pltpu.SMEM(cohort.shape, jnp.int32),
            pltpu.SMEM(site_gain.shape, f32),
            pltpu.VMEM((planes + 2, ny, nx), f32),
            pltpu.VMEM((subj, comps, planes + 2, ny, nx), f32),
            pltpu.VMEM((subj, planes, ny, nx), images.dtype),
            pltpu.VMEM((planes, ny, nx), jnp.int32),
            pltpu.VMEM((comps, planes, ny, nx), f32),
            pltpu.VMEM((planes, ny, nx), f32),
            pltpu.VMEM((subj, planes, ny, nx), f32),
            pltpu.VMEM((planes, ny, nx), f32),
            pltpu.VMEM((others, ny, nx), f32),
            dma((5,)), dma((planes,)), dma((planes,)),
            dma((2,)), dma((2,)), dma((2,)), dma((2,)),
            dma((planes,)), dma((others,)), dma((others,)), dma((others,)),
        ],
        compiler_params=pltpu.CompilerParams(
            collective_id=0, has_side_effects=True, vmem_limit_bytes=40 * 2**20
        ),
        cost_estimate=pl.CostEstimate(
            flops=24 * size, bytes_accessed=9 * size, transcendentals=0
        ),
    )(
        *(
            pltpu.with_memory_space_constraint(x, pltpu.HBM)
            for x in (template, images, velocity, labels, stiffness, cohort, site_gain)
        )
    )
    return pl.pallas_call(
        handed_on,
        out_shape=(
            jax.ShapeDtypeStruct(template.shape, f32),
            jax.ShapeDtypeStruct(velocity.shape, f32),
        ),
        in_specs=[vmem] * 2,
        out_specs=(hbm, hbm),
        scratch_shapes=[dma((subj * comps + 1,))],
        compiler_params=pltpu.CompilerParams(vmem_limit_bytes=24 * 2**20),
        cost_estimate=pl.CostEstimate(flops=0, bytes_accessed=4 * size, transcendentals=0),
    )(*held)


def solution(mesh):
    placed = (
        P("slab", None, None),
        P("grp", "slab", None, None),
        P("grp", None, "slab", None, None),
        P("slab", None, None),
        P(),
        P("grp"),
        P(),
    )
    return jax.shard_map(
        local,
        mesh=mesh,
        in_specs=placed,
        out_specs=(P("slab", None, None), P("grp", None, "slab", None, None)),
        check_vma=False,
    )
```

```python
import functools

import jax
import jax.numpy as jnp
from jax import lax
from jax.experimental import pallas as pl
from jax.experimental.pallas import tpu as pltpu
from jax.sharding import PartitionSpec as P

velocity_step = 0.05
template_step = 0.5
MESH = pl.DeviceIdType.MESH


def shifted_pair(v, axis):
    size = v.shape[axis]
    spot = lax.broadcasted_iota(jnp.int32, v.shape, axis)
    before = jnp.where(spot == 0, 0.0, pltpu.roll(v, 1, axis))
    after = jnp.where(spot == size - 1, 0.0, pltpu.roll(v, size - 1, axis))
    return before, after


def updated(z, at, vpad, slope, stiff, resid, out):
    subj, comps, _, ny, nx = vpad.shape
    rows, half = 8, nx // 2
    shape = (rows, half)
    row = lax.broadcasted_iota(jnp.int32, shape, 0)
    column = lax.broadcasted_iota(jnp.int32, shape, 1)
    sides = (pl.ds(0, half), pl.ds(half, half))
    none = jnp.zeros(shape, jnp.float32)
    for y in range(0, ny, rows):
        block = pl.ds(y, rows)
        stiffs = [stiff[z, block, side] for side in sides]
        keeps = [1.0 - 6.0 * k for k in stiffs]
        slopes = [[slope[c, z, block, side] for side in sides] for c in range(comps)]
        for s in range(subj):
            r = [resid[s, z, block, side] for side in sides]
            for c in range(comps):
                v = [vpad[s, c, z + 1, block, side] for side in sides]
                right = [pltpu.roll(x, 1, 1) for x in v]
                left = [pltpu.roll(x, half - 1, 1) for x in v]
                before = [jnp.where(column == 0, x, w) for x, w in zip((none, right[0]), right)]
                after = [
                    jnp.where(column == half - 1, x, w) for x, w in zip((left[1], none), left)
                ]
                for h, side in enumerate(sides):
                    above = vpad[s, c, z + 1, pl.ds(y - rows, rows), side] if y else none
                    below = vpad[s, c, z + 1, pl.ds(y + rows, rows), side] if y + rows < ny else none
                    up = pltpu.roll(jnp.where(row == rows - 1, above, v[h]), 1, 0)
                    down = pltpu.roll(jnp.where(row == 0, below, v[h]), rows - 1, 0)
                    beside = vpad[s, c, z, block, side] + vpad[s, c, z + 2, block, side]
                    beside = (beside + (up + down)) + (before[h] + after[h])
                    out[s, c, at, block, side] = (
                        keeps[h] * v[h] - r[h] * slopes[c][h] + stiffs[h] * beside
                    )


def kernel(
    groups, slabs, split,
    template, images, velocity, labels, stiffness_in, cohort_in, site_gain_in,
    new_template, moved, vpad, slope, stiff, resid,
    stiffness, cohort, site_gain,
    tpad, img, lab, part, got,
    load_sem, vload_sem, iload_sem,
    tsend, trecv, vsend, vrecv, rs_send, rs_recv, ag_send, ag_recv,
):
    subj, comps, planes, ny, nx = velocity.shape
    share = planes // groups
    me, at = lax.axis_index("grp"), lax.axis_index("slab")
    has_low, has_high = at > 0, at < slabs - 1
    relay = groups == 4 and share == 2
    first = lax.rem(me + 1, groups) * share
    beside_x, beside_y, across = me + 1 - 2 * lax.rem(me, 2), lax.rem(me + 2, 4), 3 - me
    hops = [
        (2 * across, beside_x), (2 * across + 1, beside_y),
        (2 * beside_x, beside_x), (2 * beside_y + 1, beside_y),
        (2 * beside_x + 1, beside_x), (2 * beside_y, beside_y),
    ]
    order = [z for z, _ in hops] + [2 * me, 2 * me + 1]
    gathers = [
        (2 * me, beside_x), (2 * me + 1, beside_y),
        (2 * me + 1, beside_x), (2 * me, beside_y),
        (2 * beside_x, beside_y), (2 * beside_y + 1, beside_x),
    ]
    arrivals = [
        (2 * beside_x, beside_x), (2 * beside_y + 1, beside_y),
        (2 * beside_x + 1, beside_x), (2 * beside_y, beside_y),
        (2 * across, beside_y), (2 * across + 1, beside_x),
    ]

    def ordered(i):
        return lax.rem(first + i, planes)

    def tload():
        return pltpu.make_async_copy(template, tpad.at[pl.ds(1, planes)], load_sem.at[0])

    def lload():
        return pltpu.make_async_copy(labels, lab, load_sem.at[1])

    def vload(z):
        return pltpu.make_async_copy(velocity.at[:, :, z], vpad.at[:, :, z + 1], vload_sem.at[z])

    def iload(z):
        return pltpu.make_async_copy(images.at[:, z], img.at[:, z], iload_sem.at[z])

    def scalar_loads():
        pairs = ((stiffness_in, stiffness), (cohort_in, cohort), (site_gain_in, site_gain))
        return [pltpu.make_async_copy(a, b, load_sem.at[2 + i]) for i, (a, b) in enumerate(pairs)]

    tload().start()
    lload().start()
    for load in scalar_loads():
        load.start()

    for i in range(planes):
        z = order[i] if relay else ordered(i)
        vload(z).start()
        iload(z).start()

    barrier = pltpu.get_barrier_semaphore()

    @pl.when(has_low)
    def _():
        pl.semaphore_signal(barrier, inc=1, device_id={"slab": at - 1}, device_id_type=MESH)

    @pl.when(has_high)
    def _():
        pl.semaphore_signal(barrier, inc=1, device_id={"slab": at + 1}, device_id_type=MESH)

    for d in range(1, groups):
        pl.semaphore_signal(
            barrier, inc=1, device_id={"grp": lax.rem(me + d, groups)}, device_id_type=MESH
        )
    pl.semaphore_wait(
        barrier, groups - 1 + has_low.astype(jnp.int32) + has_high.astype(jnp.int32)
    )

    def to_low(src, dst, send, recv):
        return pltpu.make_async_remote_copy(
            src_ref=src, dst_ref=dst, send_sem=send.at[0], recv_sem=recv.at[0],
            device_id={"slab": at - 1}, device_id_type=MESH,
        )

    def to_high(src, dst, send, recv):
        return pltpu.make_async_remote_copy(
            src_ref=src, dst_ref=dst, send_sem=send.at[1], recv_sem=recv.at[1],
            device_id={"slab": at + 1}, device_id_type=MESH,
        )

    last = planes - 1
    tlow = functools.partial(to_low, template.at[0], tpad.at[planes + 1], tsend, trecv)
    thigh = functools.partial(to_high, template.at[last], tpad.at[0], tsend, trecv)
    vlow = functools.partial(
        to_low, velocity.at[:, :, 0], vpad.at[:, :, planes + 1], vsend, vrecv
    )
    vhigh = functools.partial(
        to_high, velocity.at[:, :, last], vpad.at[:, :, 0], vsend, vrecv
    )

    @pl.when(has_low)
    def _():
        tlow().start()
        vlow().start()

    @pl.when(has_high)
    def _():
        thigh().start()
        vhigh().start()

    @pl.when(jnp.logical_not(has_low))
    def _():
        tpad[0] = jnp.zeros((ny, nx), jnp.float32)
        vpad[:, :, 0] = jnp.zeros((subj, comps, ny, nx), jnp.float32)

    @pl.when(jnp.logical_not(has_high))
    def _():
        tpad[planes + 1] = jnp.zeros((ny, nx), jnp.float32)
        vpad[:, :, planes + 1] = jnp.zeros((subj, comps, ny, nx), jnp.float32)

    tload().wait()
    lload().wait()
    for load in scalar_loads():
        load.wait()

    @pl.loop(0, planes)
    def _(z):
        t = tpad[z + 1]
        for axis in (0, 1):
            before, after = shifted_pair(t, axis)
            slope[1 + axis, z] = 0.5 * (after - before)
        level = lab[z]
        k = jnp.zeros((ny, nx), jnp.float32)
        for i in range(stiffness.shape[0]):
            k = jnp.where(level == i, velocity_step * stiffness[i], k)
        stiff[z] = k

    @pl.when(has_high)
    def _():
        to_low(template.at[0], tpad.at[planes + 1], tsend, trecv).wait_recv()

    @pl.when(has_low)
    def _():
        to_high(template.at[last], tpad.at[0], tsend, trecv).wait_recv()

    gains = [site_gain[cohort[s]] for s in range(subj)]

    def rs_copy(z, owner, slot):
        return pltpu.make_async_remote_copy(
            src_ref=part.at[z], dst_ref=got.at[slot * share + lax.rem(z, share)],
            send_sem=rs_send.at[z], recv_sem=rs_recv.at[slot * share + lax.rem(z, share)],
            device_id={"grp": owner}, device_id_type=MESH,
        )

    rows = 16

    def residual_plane(z):
        vload(z).wait()
        iload(z).wait()
        for y in range(0, ny, rows):
            block = pl.ds(y, rows)
            along_z = 0.5 * (tpad[z + 2, block] - tpad[z, block])
            slope[0, z, block] = along_z
            slopes = [along_z] + [slope[c, z, block] for c in range(1, comps)]
            t = tpad[z + 1, block]
            total = None
            for s in range(subj):
                r = t - gains[s] * img[s, z, block].astype(jnp.float32)
                for c in range(comps):
                    r = r + slopes[c] * vpad[s, c, z + 1, block]
                resid[s, z, block] = velocity_step * r
                total = r if total is None else total + r
            part[z, block] = total

    def hop(i, src, dst, peer, send, recv):
        return pltpu.make_async_remote_copy(
            src_ref=src, dst_ref=dst, send_sem=send.at[i], recv_sem=recv.at[i],
            device_id={"grp": peer}, device_id_type=MESH,
        )

    def reduce_hop(i):
        z, peer = hops[i]
        return hop(i, part.at[z], got.at[i], peer, rs_send, rs_recv)

    def gather_hop(i):
        z, peer = gathers[i]
        return hop(i, new_template.at[z], new_template.at[z], peer, ag_send, ag_recv)

    def gather_arrival(i):
        z, peer = arrivals[i]
        return hop(i, new_template.at[z], new_template.at[z], peer, ag_send, ag_recv)

    if relay:
        for i, z in enumerate(order):
            residual_plane(z)
            if i < 4:
                reduce_hop(i).start()
        for i, via in ((4, 1), (5, 0)):
            z = hops[i][0]
            reduce_hop(via).wait_recv()
            part[z] = part[z] + got[via]
            reduce_hop(i).start()
    else:
        @pl.loop(0, planes)
        def _(i):
            z = ordered(i)
            residual_plane(z)
            owner = lax.div(z, share)

            @pl.when(owner != me)
            def _():
                rs_copy(z, owner, lax.rem(me - owner + groups, groups) - 1).start()

    def update(z):
        updated(z, z, vpad, slope, stiff, resid, moved)

    @pl.loop(1, split)
    def _(z):
        update(z)

    subjects = subj * groups

    def ag_copy(j, d):
        peer = lax.rem(me + d, groups)
        slot = groups - d - 1
        return pltpu.make_async_remote_copy(
            src_ref=new_template.at[me * share + j], dst_ref=new_template.at[me * share + j],
            send_sem=ag_send.at[j * (groups - 1) + d - 1], recv_sem=ag_recv.at[slot * share + j],
            device_id={"grp": peer}, device_id_type=MESH,
        )

    def ag_arrival(j, slot):
        sender = lax.rem(me + slot + 1, groups)
        return pltpu.make_async_remote_copy(
            src_ref=new_template.at[sender * share + j], dst_ref=new_template.at[sender * share + j],
            send_sem=ag_send.at[j], recv_sem=ag_recv.at[slot * share + j],
            device_id={"grp": sender}, device_id_type=MESH,
        )

    if relay:
        for j, sources in ((0, (2, 5)), (1, (3, 4))):
            z = 2 * me + j
            total = part[z]
            for i in sources:
                reduce_hop(i).wait_recv()
                total = total + got[i]
            new_template[z] = tpad[z + 1] - (template_step / subjects) * total
            gather_hop(j).start()
        gather_hop(2).start()
        gather_hop(3).start()
    else:
        for j in range(share):
            z = me * share + j
            total = part[z]
            for slot in range(groups - 1):
                rs_copy(z, lax.rem(me + 1, groups), slot).wait_recv()
                total = total + got[slot * share + j]
            new_template[z] = tpad[z + 1] - (template_step / subjects) * total
            for d in range(1, groups):
                ag_copy(j, d).start()

    @pl.loop(split, last)
    def _(z):
        update(z)

    if relay:
        for i in (0, 1):
            gather_arrival(i).wait_recv()
            gather_hop(i + 4).start()

    @pl.when(has_low)
    def _():
        vhigh().wait_recv()

    @pl.when(has_high)
    def _():
        vlow().wait_recv()

    @pl.when(has_low)
    def _():
        tlow().wait_send()
        vlow().wait_send()

    @pl.when(has_high)
    def _():
        thigh().wait_send()
        vhigh().wait_send()

    if relay:
        for i in range(6):
            reduce_hop(i).wait_send()
            gather_hop(i).wait_send()
        for i in range(2, 6):
            gather_arrival(i).wait_recv()
    else:
        @pl.loop(0, planes)
        def _(z):
            owner = lax.div(z, share)

            @pl.when(owner != me)
            def _():
                rs_copy(z, owner, lax.rem(me - owner + groups, groups) - 1).wait_send()

        for j in range(share):
            for d in range(1, groups):
                ag_copy(j, d).wait_send()
                ag_arrival(j, d - 1).wait_recv()


def handed_on(
    template, velocity, vpad, slope, stiff, resid, new_template, new_velocity, outer, sem, outer_sem
):
    subj, comps, planes = velocity.shape[:3]
    inner = pl.ds(1, planes - 2)
    copies = [
        pltpu.make_async_copy(
            velocity.at[s, c, inner], new_velocity.at[s, c, inner], sem.at[s * comps + c]
        )
        for s in range(subj)
        for c in range(comps)
    ]
    copies.append(pltpu.make_async_copy(template, new_template, sem.at[subj * comps]))
    for copy in copies:
        copy.start()

    def outer_copy(i):
        return pltpu.make_async_copy(
            outer.at[:, :, i], new_velocity.at[:, :, i * (planes - 1)], outer_sem.at[i]
        )

    @pl.loop(0, 2)
    def _(i):
        updated(i * (planes - 1), i, vpad, slope, stiff, resid, outer)
        outer_copy(i).start()

    for copy in copies:
        copy.wait()
    for i in range(2):
        outer_copy(i).wait()


def local(template, images, velocity, labels, stiffness, cohort, site_gain):
    groups, slabs = lax.axis_size("grp"), lax.axis_size("slab")
    subj, comps, planes, ny, nx = velocity.shape
    others = (groups - 1) * (planes // groups)
    f32, dma = jnp.float32, pltpu.SemaphoreType.DMA
    hbm = pl.BlockSpec(memory_space=pltpu.HBM)
    vmem = pl.BlockSpec(memory_space=pltpu.VMEM)
    size = velocity.size
    held = pl.pallas_call(
        functools.partial(kernel, groups, slabs, planes // 2 + 1),
        out_shape=(
            pltpu.VMEM(template.shape, f32),
            pltpu.VMEM(velocity.shape, f32),
            pltpu.VMEM((subj, comps, planes + 2, ny, nx), f32),
            pltpu.VMEM((comps, planes, ny, nx), f32),
            pltpu.VMEM((planes, ny, nx), f32),
            pltpu.VMEM((subj, planes, ny, nx), f32),
        ),
        in_specs=[hbm] * 7,
        out_specs=(vmem,) * 6,
        scratch_shapes=[
            pltpu.SMEM(stiffness.shape, f32),
            pltpu.SMEM(cohort.shape, jnp.int32),
            pltpu.SMEM(site_gain.shape, f32),
            pltpu.VMEM((planes + 2, ny, nx), f32),
            pltpu.VMEM((subj, planes, ny, nx), images.dtype),
            pltpu.VMEM((planes, ny, nx), jnp.int32),
            pltpu.VMEM((planes, ny, nx), f32),
            pltpu.VMEM((others, ny, nx), f32),
            dma((5,)), dma((planes,)), dma((planes,)),
            dma((2,)), dma((2,)), dma((2,)), dma((2,)),
            dma((planes,)), dma((others,)), dma((others,)), dma((others,)),
        ],
        compiler_params=pltpu.CompilerParams(
            collective_id=0, has_side_effects=True, vmem_limit_bytes=16 * 2**20
        ),
        cost_estimate=pl.CostEstimate(
            flops=24 * size, bytes_accessed=9 * size, transcendentals=0
        ),
    )(
        *(
            pltpu.with_memory_space_constraint(x, pltpu.HBM)
            for x in (template, images, velocity, labels, stiffness, cohort, site_gain)
        )
    )
    return pl.pallas_call(
        handed_on,
        out_shape=(
            jax.ShapeDtypeStruct(template.shape, f32),
            jax.ShapeDtypeStruct(velocity.shape, f32),
        ),
        in_specs=[vmem] * 6,
        out_specs=(hbm, hbm),
        scratch_shapes=[
            pltpu.VMEM((subj, comps, 2, ny, nx), f32),
            dma((subj * comps + 1,)),
            dma((2,)),
        ],
        compiler_params=pltpu.CompilerParams(vmem_limit_bytes=8 * 2**20),
        cost_estimate=pl.CostEstimate(flops=0, bytes_accessed=4 * size, transcendentals=0),
    )(*held)


def solution(mesh):
    placed = (
        P("slab", None, None),
        P("grp", "slab", None, None),
        P("grp", None, "slab", None, None),
        P("slab", None, None),
        P(),
        P("grp"),
        P(),
    )
    return jax.shard_map(
        local,
        mesh=mesh,
        in_specs=placed,
        out_specs=(P("slab", None, None), P("grp", None, "slab", None, None)),
        check_vma=False,
    )
```

```python
import functools

import jax
import jax.numpy as jnp
from jax import lax
from jax.experimental import pallas as pl
from jax.experimental.pallas import tpu as pltpu
from jax.sharding import PartitionSpec as P

velocity_step = 0.05
template_step = 0.5
MESH = pl.DeviceIdType.MESH


def shifted_pair(v, axis):
    size = v.shape[axis]
    spot = lax.broadcasted_iota(jnp.int32, v.shape, axis)
    before = jnp.where(spot == 0, 0.0, pltpu.roll(v, 1, axis))
    after = jnp.where(spot == size - 1, 0.0, pltpu.roll(v, size - 1, axis))
    return before, after


def kernel(
    groups, slabs, split,
    template, images, velocity, labels, stiffness_in, cohort_in, site_gain_in,
    new_template, moved,
    stiffness, cohort, site_gain,
    tpad, vpad, img, lab, slope, stiff, resid, part, got,
    load_sem, vload_sem, iload_sem,
    tsend, trecv, vsend, vrecv, rs_send, rs_recv, ag_send, ag_recv,
):
    subj, comps, planes, ny, nx = velocity.shape
    share = planes // groups
    me, at = lax.axis_index("grp"), lax.axis_index("slab")
    has_low, has_high = at > 0, at < slabs - 1
    first = lax.rem(me + 1, groups) * share

    def ordered(i):
        return lax.rem(first + i, planes)

    def tload():
        return pltpu.make_async_copy(template, tpad.at[pl.ds(1, planes)], load_sem.at[0])

    def lload():
        return pltpu.make_async_copy(labels, lab, load_sem.at[1])

    def vload(z):
        return pltpu.make_async_copy(velocity.at[:, :, z], vpad.at[:, :, z + 1], vload_sem.at[z])

    def iload(z):
        return pltpu.make_async_copy(images.at[:, z], img.at[:, z], iload_sem.at[z])

    def scalar_loads():
        pairs = ((stiffness_in, stiffness), (cohort_in, cohort), (site_gain_in, site_gain))
        return [pltpu.make_async_copy(a, b, load_sem.at[2 + i]) for i, (a, b) in enumerate(pairs)]

    tload().start()
    lload().start()
    for load in scalar_loads():
        load.start()

    @pl.loop(0, planes)
    def _(i):
        z = ordered(i)
        vload(z).start()
        iload(z).start()

    barrier = pltpu.get_barrier_semaphore()

    @pl.when(has_low)
    def _():
        pl.semaphore_signal(barrier, inc=1, device_id={"slab": at - 1}, device_id_type=MESH)

    @pl.when(has_high)
    def _():
        pl.semaphore_signal(barrier, inc=1, device_id={"slab": at + 1}, device_id_type=MESH)

    for d in range(1, groups):
        pl.semaphore_signal(
            barrier, inc=1, device_id={"grp": lax.rem(me + d, groups)}, device_id_type=MESH
        )
    pl.semaphore_wait(
        barrier, groups - 1 + has_low.astype(jnp.int32) + has_high.astype(jnp.int32)
    )

    def to_low(src, dst, send, recv):
        return pltpu.make_async_remote_copy(
            src_ref=src, dst_ref=dst, send_sem=send.at[0], recv_sem=recv.at[0],
            device_id={"slab": at - 1}, device_id_type=MESH,
        )

    def to_high(src, dst, send, recv):
        return pltpu.make_async_remote_copy(
            src_ref=src, dst_ref=dst, send_sem=send.at[1], recv_sem=recv.at[1],
            device_id={"slab": at + 1}, device_id_type=MESH,
        )

    last = planes - 1
    tlow = functools.partial(to_low, template.at[0], tpad.at[planes + 1], tsend, trecv)
    thigh = functools.partial(to_high, template.at[last], tpad.at[0], tsend, trecv)
    def vlow(s):
        return to_low(
            velocity.at[s, :, 0], vpad.at[s, :, planes + 1], vsend.at[s], vrecv.at[s]
        )

    def vhigh(s):
        return to_high(
            velocity.at[s, :, last], vpad.at[s, :, 0], vsend.at[s], vrecv.at[s]
        )

    @pl.when(has_low)
    def _():
        tlow().start()
        for s in range(subj):
            vlow(s).start()

    @pl.when(has_high)
    def _():
        thigh().start()
        for s in range(subj):
            vhigh(s).start()

    @pl.when(jnp.logical_not(has_low))
    def _():
        tpad[0] = jnp.zeros((ny, nx), jnp.float32)
        vpad[:, :, 0] = jnp.zeros((subj, comps, ny, nx), jnp.float32)

    @pl.when(jnp.logical_not(has_high))
    def _():
        tpad[planes + 1] = jnp.zeros((ny, nx), jnp.float32)
        vpad[:, :, planes + 1] = jnp.zeros((subj, comps, ny, nx), jnp.float32)

    tload().wait()
    lload().wait()
    for load in scalar_loads():
        load.wait()

    @pl.loop(0, planes)
    def _(z):
        t = tpad[z + 1]
        for axis in (0, 1):
            before, after = shifted_pair(t, axis)
            slope[1 + axis, z] = 0.5 * (after - before)
        level = lab[z]
        k = jnp.zeros((ny, nx), jnp.float32)
        for i in range(stiffness.shape[0]):
            k = jnp.where(level == i, velocity_step * stiffness[i], k)
        stiff[z] = k

    @pl.when(has_high)
    def _():
        to_low(template.at[0], tpad.at[planes + 1], tsend, trecv).wait_recv()

    @pl.when(has_low)
    def _():
        to_high(template.at[last], tpad.at[0], tsend, trecv).wait_recv()

    gains = [site_gain[cohort[s]] for s in range(subj)]

    def rs_copy(z, owner, slot):
        return pltpu.make_async_remote_copy(
            src_ref=part.at[z], dst_ref=got.at[slot, lax.rem(z, share)],
            send_sem=rs_send.at[z], recv_sem=rs_recv.at[slot, lax.rem(z, share)],
            device_id={"grp": owner}, device_id_type=MESH,
        )

    rows = 16

    @pl.loop(0, planes)
    def _(i):
        z = ordered(i)
        vload(z).wait()
        iload(z).wait()
        for y in range(0, ny, rows):
            block = pl.ds(y, rows)
            along_z = 0.5 * (tpad[z + 2, block] - tpad[z, block])
            slope[0, z, block] = along_z
            slopes = [along_z] + [slope[c, z, block] for c in range(1, comps)]
            t = tpad[z + 1, block]
            total = None
            for s in range(subj):
                r = t - gains[s] * img[s, z, block].astype(jnp.float32)
                for c in range(comps):
                    r = r + slopes[c] * vpad[s, c, z + 1, block]
                resid[s, z, block] = r
                total = r if total is None else total + r
            part[z, block] = total
        owner = lax.div(z, share)

        @pl.when(owner != me)
        def _():
            rs_copy(z, owner, lax.rem(me - owner + groups, groups) - 1).start()

    def update(z):
        k = stiff[z]
        keep = 1.0 - 6.0 * k
        push = [velocity_step * slope[c, z] for c in range(comps)]

        @pl.loop(0, subj)
        def _(s):
            r = resid[s, z]
            for c in range(comps):
                v = vpad[s, c, z + 1]
                up, down = shifted_pair(v, 0)
                left, right = shifted_pair(v, 1)
                beside = (vpad[s, c, z] + vpad[s, c, z + 2]) + ((up + down) + (left + right))
                moved[s, c, z] = keep * v - r * push[c] + k * beside


    @pl.loop(1, split)
    def _(z):
        update(z)

    subjects = subj * groups

    def ag_copy(j, d):
        peer = lax.rem(me + d, groups)
        slot = groups - d - 1
        return pltpu.make_async_remote_copy(
            src_ref=new_template.at[me * share + j], dst_ref=new_template.at[me * share + j],
            send_sem=ag_send.at[j, d - 1], recv_sem=ag_recv.at[slot, j],
            device_id={"grp": peer}, device_id_type=MESH,
        )

    def ag_arrival(j, slot):
        sender = lax.rem(me + slot + 1, groups)
        return pltpu.make_async_remote_copy(
            src_ref=new_template.at[sender * share + j], dst_ref=new_template.at[sender * share + j],
            send_sem=ag_send.at[j, 0], recv_sem=ag_recv.at[slot, j],
            device_id={"grp": sender}, device_id_type=MESH,
        )

    for j in range(share):
        z = me * share + j
        total = part[z]
        for slot in range(groups - 1):
            rs_copy(z, lax.rem(me + 1, groups), slot).wait_recv()
            total = total + got[slot, j]
        new_template[z] = tpad[z + 1] - (template_step / subjects) * total
        for d in range(1, groups):
            ag_copy(j, d).start()

    @pl.loop(split, last)
    def _(z):
        update(z)

    @pl.when(has_low)
    def _():
        for s in range(subj):
            vhigh(s).wait_recv()

    update(0)

    @pl.when(has_high)
    def _():
        for s in range(subj):
            vlow(s).wait_recv()

    update(last)

    @pl.when(has_low)
    def _():
        tlow().wait_send()
        for s in range(subj):
            vlow(s).wait_send()

    @pl.when(has_high)
    def _():
        thigh().wait_send()
        for s in range(subj):
            vhigh(s).wait_send()

    @pl.loop(0, planes)
    def _(z):
        owner = lax.div(z, share)

        @pl.when(owner != me)
        def _():
            rs_copy(z, owner, lax.rem(me - owner + groups, groups) - 1).wait_send()

    for j in range(share):
        for d in range(1, groups):
            ag_copy(j, d).wait_send()
            ag_arrival(j, d - 1).wait_recv()


def handed_on(template, velocity, new_template, new_velocity, sem):
    copies = [
        pltpu.make_async_copy(velocity, new_velocity, sem.at[0]),
        pltpu.make_async_copy(template, new_template, sem.at[1]),
    ]
    for copy in copies:
        copy.start()
    for copy in copies:
        copy.wait()


def local(template, images, velocity, labels, stiffness, cohort, site_gain):
    groups, slabs = lax.axis_size("grp"), lax.axis_size("slab")
    subj, comps, planes, ny, nx = velocity.shape
    share = planes // groups
    f32, dma = jnp.float32, pltpu.SemaphoreType.DMA
    hbm = pl.BlockSpec(memory_space=pltpu.HBM)
    vmem = pl.BlockSpec(memory_space=pltpu.VMEM)
    size = velocity.size
    held = pl.pallas_call(
        functools.partial(kernel, groups, slabs, planes // 2 + 1),
        out_shape=(
            pltpu.VMEM(template.shape, f32),
            pltpu.VMEM(velocity.shape, f32),
        ),
        in_specs=[hbm] * 7,
        out_specs=(vmem, vmem),
        scratch_shapes=[
            pltpu.SMEM(stiffness.shape, f32),
            pltpu.SMEM(cohort.shape, jnp.int32),
            pltpu.SMEM(site_gain.shape, f32),
            pltpu.VMEM((planes + 2, ny, nx), f32),
            pltpu.VMEM((subj, comps, planes + 2, ny, nx), f32),
            pltpu.VMEM((subj, planes, ny, nx), images.dtype),
            pltpu.VMEM((planes, ny, nx), jnp.int32),
            pltpu.VMEM((comps, planes, ny, nx), f32),
            pltpu.VMEM((planes, ny, nx), f32),
            pltpu.VMEM((subj, planes, ny, nx), f32),
            pltpu.VMEM((planes, ny, nx), f32),
            pltpu.VMEM((groups - 1, share, ny, nx), f32),
            dma((5,)), dma((planes,)), dma((planes,)),
            dma((2,)), dma((2,)), dma((subj, 2)), dma((subj, 2)),
            dma((planes,)), dma((groups - 1, share)),
            dma((share, groups - 1)), dma((groups - 1, share)),
        ],
        compiler_params=pltpu.CompilerParams(
            collective_id=0, has_side_effects=True, vmem_limit_bytes=40 * 2**20
        ),
        cost_estimate=pl.CostEstimate(
            flops=24 * size, bytes_accessed=9 * size, transcendentals=0
        ),
    )(
        *(
            pltpu.with_memory_space_constraint(x, pltpu.HBM)
            for x in (template, images, velocity, labels, stiffness, cohort, site_gain)
        )
    )
    return pl.pallas_call(
        handed_on,
        out_shape=(
            jax.ShapeDtypeStruct(template.shape, f32),
            jax.ShapeDtypeStruct(velocity.shape, f32),
        ),
        in_specs=[vmem] * 2,
        out_specs=(hbm, hbm),
        scratch_shapes=[dma((2,))],
        compiler_params=pltpu.CompilerParams(vmem_limit_bytes=24 * 2**20),
        cost_estimate=pl.CostEstimate(flops=0, bytes_accessed=4 * size, transcendentals=0),
    )(*held)


def solution(mesh):
    placed = (
        P("slab", None, None),
        P("grp", "slab", None, None),
        P("grp", None, "slab", None, None),
        P("slab", None, None),
        P(),
        P("grp"),
        P(),
    )
    return jax.shard_map(
        local,
        mesh=mesh,
        in_specs=placed,
        out_specs=(P("slab", None, None), P("grp", None, "slab", None, None)),
        check_vma=False,
    )
```
